32 devices in a mesh: refl: 4 (over y, core), atom: 8 (over z, x).
Axes of the slice: x: 2, y: 2, z: 4, core: 2. Of those that a mesh axis runs over, the one named last changes fastest.
Arguments:
- features: bfloat16 [16384, 128], P('atom'), may hold values from -6 to 6
- ln_gain: float32 [2, 128], replicated, may hold values from 0.25 to 1.75
- w_qkv: bfloat16 [2, 3, 128, 128], P(None, None, None, 'refl'), may hold values from -0.5 to 0.5
- w_out: bfloat16 [2, 128, 128], replicated, may hold values from -0.5 to 0.5
- w_coord: bfloat16 [3, 128], replicated, may hold values from -0.5 to 0.5
- noisy_coords: float32 [3, 16384], P(None, 'atom'), may hold values from 0 to 1
- scatter_power: float32 [16384], P('atom'), may hold values from 0.5 to 4
- route: int32 [8, 8], P('atom'), may hold values from 0 to 7, each once within a row
- miller: int32 [3, 4096], P(None, 'refl'), may hold values from -12 to 12
- rotations: int32 [4, 3, 3], replicated, may hold values from -1 to 1, as said below
- shifts: float32 [4, 3], replicated, may hold values from 0 to 1
- observed: float32 [4096], P('refl'), may hold values from 0.3 to 3
- obs_weight: float32 [4096], P('refl'), may hold values from 0.2 to 2
Outputs:
- atom_out: bfloat16 [16384, 128], P('atom')
- amplitude: float32 [4096], P(('refl', 'atom'))
- coord_grad: float32 [3, 16384], P(None, 'atom')
The draws below stay inside these ranges and needn't reach their ends.
Inputs may be any that keep to these rules, and one draw needn't show every extreme that they name: Each row of route names every block of a shard once. `rotations`: each of the 4 matrices is a permutation matrix with signs.
All inputs are finite; a program needn't handle non-finite values.
Results may differ from the reference program's by a relative error of at most 0.012.
Values may be sent and summed in bfloat16 or wider, within the bound.
A program may use at most 64 MiB of HBM per device.

```python
import math
import jax
import jax.numpy as jnp
from jax import lax

C = 128
HEAD_FEATURES = 32
QWIN = 32
WINDOW_KEYS = 128
LAYERS = 2
NOPS = 4
ATOM_DEV = 2048
NATOM = 16384
NREFL = 4096
SLOTS = 8


def draw_rotations(key, part):
    keys = jax.random.split(jax.random.fold_in(key, 71), NOPS)
    perms = jnp.stack([jax.random.permutation(keys[s], 3) for s in range(NOPS)])
    signs = jax.random.randint(jax.random.fold_in(key, 72), (NOPS, 3), 0, 2) * 2 - 1
    columns = jnp.arange(3, dtype=jnp.int32)
    onehot = (perms[:, :, None] == columns[None, None, :]).astype(jnp.int32)
    return (onehot * signs[:, :, None]).astype(jnp.int32)


def plant(entries, own_key, least, top_value):
    spot = [jax.random.randint(jax.random.fold_in(own_key, axis), (), 0, length) for axis, length in enumerate(entries.shape)]
    longest = entries.shape.index(max(entries.shape))
    neighbour = spot[:longest] + [(spot[longest] + 1) % entries.shape[longest]] + spot[longest + 1:]
    return entries.at[tuple(spot)].set(least).at[tuple(neighbour)].set(top_value)


def level_of(key, dims, cuts, least, largest):
    factor_of = 1.0
    for axis_at, blocks in cuts:
        steps = jax.random.uniform(jax.random.fold_in(jax.random.fold_in(key, 6), axis_at), (blocks,), jnp.float32, least / len(cuts), largest / len(cuts))
        factor_of = factor_of * jnp.repeat(jnp.exp(steps), dims[axis_at] // blocks).reshape((-1,) + (1,) * (len(dims) - 1 - axis_at))
    return factor_of


def bell_draw(key, dims, width, limit, cuts=(), held_as=jnp.bfloat16):
    entries = jax.random.normal(key, dims, jnp.float32) * width
    if len(cuts) > 0:
        entries = level_of(key, dims, cuts, -0.22, 0.18) * entries
    return jnp.clip(entries, min=-limit, max=limit).astype(held_as)


def setup_inputs(seed: int = 0) -> dict:
    key_list = jax.random.split(jax.random.key(seed), 14)
    return {
        "features": bell_draw(key_list[0], (NATOM, C), 1.0, 6.0, ((0, 8),)),
        "ln_gain": jnp.clip(1.0 + 0.15 * jax.random.normal(key_list[1], (LAYERS, C), jnp.float32), 0.25, 1.75),
        "w_qkv": bell_draw(key_list[2], (LAYERS, 3, C, C), C ** -0.5, 0.5, ((3, 4),)),
        "w_out": bell_draw(key_list[3], (LAYERS, C, C), C ** -0.5, 0.5),
        "w_coord": bell_draw(key_list[4], (3, C), C ** -0.5, 0.5),
        "noisy_coords": jnp.clip(1.0 * jax.random.uniform(key_list[5], (3, NATOM), jnp.float32) ** level_of(key_list[5], (3, NATOM), ((1, 8),), -0.2, 0.2), 0.0, 1.0),
        "scatter_power": jnp.clip(jnp.exp(math.log(4.0) - 2.0794415 * jax.random.uniform(key_list[6], (NATOM,), jnp.float32) ** level_of(key_list[6], (NATOM,), ((0, 8),), -0.2, 0.2)), 0.5, 4.0),
        "route": jax.vmap(lambda own: jax.random.permutation(own, SLOTS))(jax.random.split(key_list[7], SLOTS)).reshape((SLOTS, SLOTS)).astype(jnp.int32),
        "miller": plant(jax.random.randint(key_list[8], (3, NREFL), -12, 13), jax.random.fold_in(key_list[8], 1), -12, 12).astype(jnp.int32),
        "rotations": draw_rotations(jax.random.fold_in(key_list[13], 71), 0),
        "shifts": jnp.clip(jax.random.uniform(key_list[10], (NOPS, 3), jnp.float32, 0.0, 1.0), 0.0, 1.0),
        "observed": jnp.clip(jnp.exp(math.log(3.0) - 2.3025851 * jax.random.uniform(key_list[11], (NREFL,), jnp.float32) ** level_of(key_list[11], (NREFL,), ((0, 4),), -0.2, 0.2)), 0.3, 3.0),
        "obs_weight": jnp.clip(jnp.exp(math.log(2.0) - 2.3025851 * jax.random.uniform(key_list[12], (NREFL,), jnp.float32) ** level_of(key_list[12], (NREFL,), ((0, 4),), -0.2, 0.2)), 0.2, 2.0),
    }


def layer_norm(x, gain):
    mean = lax.optimization_barrier(jnp.mean(x, axis=-1, keepdims=True))
    cent = x - mean
    var = lax.optimization_barrier(jnp.mean(cent * cent, axis=-1, keepdims=True))
    return (cent * lax.rsqrt(var + 1e-05) * gain).astype(jnp.bfloat16)

def window_blocks(padded, window_count):
    parts = [padded[QWIN * j:QWIN * j + window_count * QWIN].reshape(window_count, QWIN, -1) for j in range(WINDOW_KEYS // QWIN)]
    return jnp.concatenate(parts, axis=1)

def attend_windowed(query_rows, padded_keys, padded_values, valid_mask):
    window_count = query_rows.shape[0] // QWIN
    head_count = query_rows.shape[1] // HEAD_FEATURES
    qwin = query_rows.reshape(window_count, QWIN, head_count, HEAD_FEATURES).astype(jnp.float32)
    kwin = window_blocks(padded_keys, window_count).reshape(window_count, WINDOW_KEYS, head_count, HEAD_FEATURES).astype(jnp.float32)
    window_values = window_blocks(padded_values, window_count).reshape(window_count, WINDOW_KEYS, head_count, HEAD_FEATURES).astype(jnp.float32)
    mwin = window_blocks(valid_mask, window_count)[..., 0]
    scores = jnp.einsum('wqhd,wkhd->whqk', qwin, kwin) * HEAD_FEATURES ** (-0.5)
    scores = jnp.where(mwin[:, None, None, :] > 0.5, scores, -1e+30)
    top = lax.optimization_barrier(jnp.max(scores, axis=-1, keepdims=True))
    expo = jnp.exp(scores - top)
    probs = (expo / lax.optimization_barrier(jnp.sum(expo, axis=-1, keepdims=True))).astype(jnp.bfloat16)
    out = jnp.einsum('whqk,wkhd->wqhd', probs.astype(jnp.float32), window_values)
    return out.reshape(window_count * QWIN, head_count * HEAD_FEATURES).astype(jnp.bfloat16)

def phases(hs_blk, tsh_blk, pos):
    turn = hs_blk[:, 0, :, None] * pos[0] + hs_blk[:, 1, :, None] * pos[1] + hs_blk[:, 2, :, None] * pos[2]
    angle = 2.0 * math.pi * (turn + tsh_blk[:, :, None])
    return (jnp.cos(angle), jnp.sin(angle))

def reference(features, ln_gain, w_qkv, w_out, w_coord, noisy_coords, scatter_power, route, miller, rotations, shifts, observed, obs_weight):
    window_border = (WINDOW_KEYS - QWIN) // 2
    x = features.astype(jnp.float32)
    place = jnp.arange(NATOM + 2 * window_border, dtype=jnp.int32) - window_border
    valid_mask = ((place >= 0) & (place < NATOM)).astype(jnp.float32)[:, None]
    for layer in range(LAYERS):
        normed = layer_norm(x, ln_gain[layer])
        query_rows = jnp.dot(normed, w_qkv[layer, 0], preferred_element_type=jnp.float32).astype(jnp.bfloat16)
        keys = jnp.dot(normed, w_qkv[layer, 1], preferred_element_type=jnp.float32).astype(jnp.bfloat16)
        value_rows = jnp.dot(normed, w_qkv[layer, 2], preferred_element_type=jnp.float32).astype(jnp.bfloat16)
        padded_keys = jnp.pad(keys, ((window_border, window_border), (0, 0)))
        padded_values = jnp.pad(value_rows, ((window_border, window_border), (0, 0)))
        head_rows = attend_windowed(query_rows, padded_keys, padded_values, valid_mask)
        x = x + jnp.dot(head_rows, w_out[layer], preferred_element_type=jnp.float32)
    atom_out = x.astype(jnp.bfloat16)
    moved = noisy_coords + 0.02 * jnp.dot(w_coord, atom_out.T, preferred_element_type=jnp.float32)
    blk = ATOM_DEV // SLOTS
    source = jnp.arange(SLOTS, dtype=jnp.int32)
    index = source[None, :, None] * ATOM_DEV + route.T.astype(jnp.int32)[:, :, None] * blk + jnp.arange(blk, dtype=jnp.int32)[None, None, :]
    index = index.reshape(-1)
    pos = moved[:, index]
    power = scatter_power[index]
    hs = jnp.einsum('skc,kr->scr', rotations.astype(jnp.float32), miller.astype(jnp.float32), precision=lax.Precision.HIGHEST)
    tsh = jnp.einsum('kr,sk->sr', miller.astype(jnp.float32), shifts, precision=lax.Precision.HIGHEST)
    norm = 1.0 / math.sqrt(NOPS * NATOM)
    rows = min(128, NREFL)
    turns = NREFL // rows
    hs_b = hs.reshape(NOPS, 3, turns, rows).transpose(2, 0, 1, 3)
    ts_b = tsh.reshape(NOPS, turns, rows).transpose(1, 0, 2)

    def forward(item):
        cosv, sinv = phases(item[0], item[1], pos)
        fa = jnp.einsum('sra,a->r', cosv, power, precision=lax.Precision.HIGHEST)
        fb = jnp.einsum('sra,a->r', sinv, power, precision=lax.Precision.HIGHEST)
        return jnp.stack([fa, fb]) * norm
    parts = lax.map(forward, (hs_b, ts_b))
    totals = parts.transpose(1, 0, 2).reshape(2, NREFL)
    amplitude = jnp.sqrt(totals[0] * totals[0] + totals[1] * totals[1] + 1.0)
    slope = 2.0 * obs_weight * (amplitude - observed) / (amplitude * math.sqrt(NREFL))
    slopes = jnp.stack([slope * totals[0], slope * totals[1]])
    sl_b = slopes.reshape(2, turns, rows).transpose(1, 0, 2)

    def backward(total, item):
        cosv, sinv = phases(item[0], item[1], pos)
        coef = 2.0 * math.pi * norm * power * (cosv * item[2][1][None, :, None] - sinv * item[2][0][None, :, None])
        return (total + jnp.einsum('scr,sra->ca', item[0], coef, precision=lax.Precision.HIGHEST), None)
    coord_grad, unused = lax.scan(backward, jnp.zeros((3, NATOM), jnp.float32), (hs_b, ts_b, sl_b))
    return (atom_out, amplitude, coord_grad)
```

```python
import functools
import math

import jax
import jax.numpy as jnp
from jax import lax
from jax.experimental import pallas as pl
from jax.experimental.pallas import tpu as pltpu
from jax.sharding import PartitionSpec as P

HEAD_FEATURES = 32
QWIN = 32
WINDOW_KEYS = 128
LAYERS = 2
BORDER = (WINDOW_KEYS - QWIN) // 2
HALO = 128
QB = 128
KB = 256
MAXH = 12
KP = 32
LP = MAXH + 1
KL = KP * LP
MESH = pl.DeviceIdType.MESH
VMEM = pl.BlockSpec(memory_space=pltpu.VMEM)
SMEM = pl.BlockSpec(memory_space=pltpu.SMEM)
VLIM = 56 * 1024 * 1024
NT = (((1,), (1,)), ((), ()))


def peers(axis):
    n = lax.axis_size(axis)
    me = lax.axis_index(axis)
    return [lax.rem(me + off, n) for off in range(1, n)]


def greet(ids):
    barrier = pltpu.get_barrier_semaphore()
    for where in ids:
        pl.semaphore_signal(barrier, inc=1, device_id=where, device_id_type=MESH)
    pl.semaphore_wait(barrier, len(ids))


def push(src, dst, send, recv, where):
    return pltpu.make_async_remote_copy(
        src_ref=src, dst_ref=dst, send_sem=send, recv_sem=recv, device_id=where, device_id_type=MESH
    )


def exchange_kernel(axis, shared, src_ref, out_ref, send, recv):
    me = lax.axis_index(axis)
    others = peers(axis)
    greet([{axis: p} for p in others])
    copies = [
        push(src_ref if shared else src_ref.at[p], out_ref.at[me], send.at[i], recv.at[i], {axis: p})
        for i, p in enumerate(others)
    ]
    for c in copies:
        c.start()
    out_ref[me] = src_ref[...] if shared else src_ref[me]
    for c in copies:
        c.wait()


def exchange(src, axis, cid, shared):
    n = lax.axis_size(axis)
    shape = ((n,) + src.shape) if shared else src.shape
    return pl.pallas_call(
        functools.partial(exchange_kernel, axis, shared),
        out_shape=jax.ShapeDtypeStruct(shape, src.dtype),
        in_specs=[VMEM],
        out_specs=VMEM,
        scratch_shapes=[pltpu.SemaphoreType.DMA((n - 1,)), pltpu.SemaphoreType.DMA((n - 1,))],
        compiler_params=pltpu.CompilerParams(collective_id=cid, has_side_effects=True, vmem_limit_bytes=VLIM),
    )(src)


def opening_kernel(w_ref, feat_ref, wg_ref, left_ref, right_ref, send, recv):
    me = lax.axis_index("refl")
    n = lax.axis_size("atom")
    at = lax.axis_index("atom")
    local = feat_ref.shape[0]
    after, before = lax.rem(at + 1, n), lax.rem(at + n - 1, n)
    others = peers("refl")
    greet([{"refl": p} for p in others] + [{"atom": after}, {"atom": before}])
    copies = [
        push(feat_ref.at[pl.ds(local - HALO, HALO)], left_ref, send.at[0], recv.at[0], {"atom": after}),
        push(feat_ref.at[pl.ds(0, HALO)], right_ref, send.at[1], recv.at[1], {"atom": before}),
    ]
    copies += [
        push(w_ref, wg_ref.at[me], send.at[2 + i], recv.at[2 + i], {"refl": p})
        for i, p in enumerate(others)
    ]
    for c in copies:
        c.start()
    wg_ref[me] = w_ref[...]
    for c in copies:
        c.wait()


def opening(wpack, features, cid):
    n = lax.axis_size("refl")
    halo = jax.ShapeDtypeStruct((HALO, features.shape[1]), features.dtype)
    return pl.pallas_call(
        opening_kernel,
        out_shape=(jax.ShapeDtypeStruct((n,) + wpack.shape, wpack.dtype), halo, halo),
        in_specs=[VMEM, VMEM],
        out_specs=(VMEM, VMEM, VMEM),
        scratch_shapes=[pltpu.SemaphoreType.DMA((n + 1,)), pltpu.SemaphoreType.DMA((n + 1,))],
        compiler_params=pltpu.CompilerParams(collective_id=cid, has_side_effects=True, vmem_limit_bytes=VLIM),
    )(wpack, features)


def layer_norm(x, gain):
    mean = jnp.mean(x, axis=-1, keepdims=True)
    cent = x - mean
    var = jnp.mean(cent * cent, axis=-1, keepdims=True)
    return (cent * lax.rsqrt(var + 1e-05) * gain).astype(jnp.bfloat16)


def attention_layer(x_ref, proj_ref, low, high, first_key, natom, band, wg_ref, gain, wout_ref, layer):
    width = x_ref.shape[1]
    per_dev = wg_ref.shape[1] // (LAYERS * width)
    normed = layer_norm(x_ref[low:high, :], gain)
    for dev in range(wg_ref.shape[0]):
        for j in range(per_dev):
            at = (j * LAYERS + layer) * width
            proj_ref[dev * per_dev + j, low:high, :] = jnp.dot(
                normed, wg_ref[dev, at : at + width, :], preferred_element_type=jnp.float32
            ).astype(jnp.bfloat16)
    lane = lax.broadcasted_iota(jnp.int32, (1, KB), 1)
    side = (KB - QB) // 2
    for b in range((high - low - 2 * side) // QB):
        keys = low + b * QB
        place = first_key + keys + lane
        bias = band + jnp.where((place >= 0) & (place < natom), 0.0, -1e30)
        mine = slice(keys + side, keys + side + QB)
        heads = []
        for h in range(proj_ref.shape[0]):
            q = proj_ref[h, mine, 0:HEAD_FEATURES]
            k = proj_ref[h, keys : keys + KB, HEAD_FEATURES : 2 * HEAD_FEATURES]
            v = proj_ref[h, keys : keys + KB, 2 * HEAD_FEATURES : 3 * HEAD_FEATURES]
            scores = lax.dot_general(q, k, NT, preferred_element_type=jnp.float32)
            scores = scores * HEAD_FEATURES ** (-0.5) + bias
            expo = jnp.exp(scores - jnp.max(scores, axis=-1, keepdims=True))
            probs = (expo * (1.0 / jnp.sum(expo, axis=-1, keepdims=True))).astype(jnp.bfloat16)
            o = jnp.dot(probs, v, preferred_element_type=jnp.float32)
            heads.append(o.astype(jnp.bfloat16))
        side_by_side = jnp.concatenate(heads, axis=1)
        x_ref[mine, :] = x_ref[mine, :] + jnp.dot(
            side_by_side, wout_ref[layer], preferred_element_type=jnp.float32
        )


def band_bias():
    a = lax.broadcasted_iota(jnp.int32, (QB, KB), 0)
    c = lax.broadcasted_iota(jnp.int32, (QB, KB), 1)
    rel = c - (KB - QB) // 2 - (a // QWIN) * QWIN
    return jnp.where((rel >= -BORDER) & (rel < WINDOW_KEYS - BORDER), 0.0, -1e30)


def attention_kernel(
    feat_ref, left_ref, right_ref, wg_ref, gain_ref, wout_ref, wc_ref, noisy_ref, power_ref,
    out_ref, packed_ref, ext_ref, x_ref, proj_ref,
):
    local = feat_ref.shape[0]
    sub = out_ref.shape[0]
    rank = lax.axis_index("atom")
    part = lax.axis_index("refl")
    natom = local * lax.axis_size("atom")
    ext_ref[0:HALO] = left_ref[...]
    ext_ref[HALO : HALO + local] = feat_ref[...]
    ext_ref[HALO + local :] = right_ref[...]
    start = pl.multiple_of(part * sub, sub)
    first = rank * local + part * sub - HALO
    band = band_bias()
    rows = sub + 2 * HALO
    x_ref[...] = ext_ref[pl.ds(start, rows), :].astype(jnp.float32)
    side = (KB - QB) // 2
    for layer in range(LAYERS):
        attention_layer(
            x_ref, proj_ref, layer * side, rows - layer * side, first, natom, band,
            wg_ref, gain_ref[layer : layer + 1, :], wout_ref, layer,
        )
    atom_out = x_ref[HALO : HALO + sub, :].astype(jnp.bfloat16)
    out_ref[...] = atom_out
    shift = lax.dot_general(wc_ref[...], atom_out, NT, preferred_element_type=jnp.float32)
    cols = pl.ds(start, sub)
    packed_ref[...] = jnp.zeros_like(packed_ref)
    packed_ref[0:3, :] = noisy_ref[:, cols] + 0.02 * shift[0:3]
    packed_ref[3:4, :] = power_ref[:, cols]


def attention(features, left, right, wg, ln_gain, w_out, w_coord, noisy, power):
    local, width = features.shape
    sub = local // lax.axis_size("refl")
    wc = jnp.pad(w_coord, ((0, 16 - w_coord.shape[0]), (0, 0)))
    return pl.pallas_call(
        attention_kernel,
        out_shape=(
            jax.ShapeDtypeStruct((sub, width), jnp.bfloat16),
            jax.ShapeDtypeStruct((8, sub), jnp.float32),
        ),
        in_specs=[VMEM] * 9,
        out_specs=(VMEM, VMEM),
        scratch_shapes=[
            pltpu.VMEM((local + 2 * HALO, width), jnp.bfloat16),
            pltpu.VMEM((sub + 2 * HALO, width), jnp.float32),
            pltpu.VMEM((wg.shape[0] * wg.shape[1] // (LAYERS * width), sub + 2 * HALO, wg.shape[2]), jnp.bfloat16),
        ],
        compiler_params=pltpu.CompilerParams(vmem_limit_bytes=VLIM),
    )(features, left, right, wg, ln_gain, w_out, wc, noisy, power[None, :])


SIN = [(-1) ** i * math.pi ** (2 * i + 1) / math.factorial(2 * i + 1) for i in range(6)]
COS = [(-1) ** i * math.pi ** (2 * i) / math.factorial(2 * i) for i in range(7)]


def circle(turns):
    r = turns - jnp.floor(turns + 0.5)
    u = r * r
    s = SIN[-1]
    for c in SIN[-2::-1]:
        s = s * u + c
    s = s * r
    c = COS[-1]
    for d in COS[-2::-1]:
        c = c * u + d
    return (1.0 - 2.0 * s * s, 2.0 * s * c)


def tables(pos_ref, cols, width):
    index = lax.broadcasted_iota(jnp.int32, (KP, width), 0).astype(jnp.float32)
    xc, xs = circle((index - MAXH) * pos_ref[0:1, cols])
    yc, ys = circle((index - MAXH) * pos_ref[1:2, cols])
    zc, zs = circle(index[0:16] * pos_ref[2:3, cols])
    return xc, xs, yc, ys, zc, zs


def operator_terms(mil_ref, rot_ref, shift_ref, s):
    mil = [mil_ref[k : k + 1, :] for k in range(3)]
    h = [sum(rot_ref[s * 9 + k * 3 + c] * mil[k] for k in range(3)) for c in range(3)]
    t = sum(mil[k].astype(jnp.float32) * shift_ref[s * 3 + k] for k in range(3))
    tc, ts = circle(t)
    flip = jnp.where(h[2] < 0, -1, 1)
    return (
        h[2] * flip * KP + h[1] * flip + MAXH,
        h[0] * flip + MAXH,
        flip.astype(jnp.float32),
        tc,
        ts,
    )


def hot(index, rows):
    return lax.broadcasted_iota(jnp.int32, (rows, index.shape[1]), 0) == index


def as_bf16(mask):
    return jnp.where(mask, 1.0, 0.0).astype(jnp.bfloat16)


def split2(x):
    hi = x.astype(jnp.bfloat16)
    return hi, (x - hi.astype(jnp.float32)).astype(jnp.bfloat16)


def forward_kernel(chunk, norm, pos_ref, mil_ref, rot_ref, shift_ref, f_ref, xt_ref, yz_ref):
    local = pos_ref.shape[1]
    group = mil_ref.shape[1]
    nops = shift_ref.shape[0] // 3

    def build(i, carry):
        cols = pl.ds(pl.multiple_of(i * chunk, chunk), chunk)
        xc, xs, yc, ys, zc, zs = tables(pos_ref, cols, chunk)
        power = pos_ref[3:4, cols]
        zc, zs = zc * power, zs * power
        xt_ref[0:KP, cols] = xc.astype(jnp.bfloat16)
        xt_ref[KP : 2 * KP, cols] = xs.astype(jnp.bfloat16)
        for l in range(LP):
            a, b = zc[l : l + 1], zs[l : l + 1]
            yz_ref[l * KP : (l + 1) * KP, cols] = (yc * a - ys * b).astype(jnp.bfloat16)
            yz_ref[KL + l * KP : KL + (l + 1) * KP, cols] = (yc * b + ys * a).astype(jnp.bfloat16)
        return carry

    lax.fori_loop(0, local // chunk, build, 0)
    xt = xt_ref[...]
    gc = lax.dot_general(xt, yz_ref[0:KL], NT, preferred_element_type=jnp.float32)
    gs = lax.dot_general(xt, yz_ref[KL:], NT, preferred_element_type=jnp.float32)
    re = gc[0:KP] - gs[KP:]
    im = gs[0:KP] + gc[KP:]
    re_hi, re_lo = split2(re)
    im_hi, im_lo = split2(im)
    grid = jnp.concatenate([re_hi, im_hi, re_lo, im_lo], axis=0)
    fa = jnp.zeros((1, group), jnp.float32)
    fb = jnp.zeros((1, group), jnp.float32)
    for s in range(nops):
        kl, h, flip, tc, ts = operator_terms(mil_ref, rot_ref, shift_ref, s)
        found = jnp.dot(grid, as_bf16(hot(kl, KL)), preferred_element_type=jnp.float32)
        pick = hot(h, KP)
        gre = jnp.sum(jnp.where(pick, found[0:KP] + found[2 * KP : 3 * KP], 0.0), axis=0, keepdims=True)
        gim = flip * jnp.sum(jnp.where(pick, found[KP : 2 * KP] + found[3 * KP :], 0.0), axis=0, keepdims=True)
        fa = fa + tc * gre - ts * gim
        fb = fb + tc * gim + ts * gre
    f_ref[0:1, :] = fa * norm
    f_ref[1:2, :] = fb * norm


def forward(pos, miller, rot, shifts, norm):
    local = pos.shape[1]
    return pl.pallas_call(
        functools.partial(forward_kernel, min(256, local), norm),
        out_shape=jax.ShapeDtypeStruct((2, miller.shape[1]), jnp.float32),
        in_specs=[VMEM, VMEM, SMEM, SMEM],
        out_specs=VMEM,
        scratch_shapes=[
            pltpu.VMEM((2 * KP, local), jnp.bfloat16),
            pltpu.VMEM((2 * KL, local), jnp.bfloat16),
        ],
        compiler_params=pltpu.CompilerParams(vmem_limit_bytes=VLIM),
    )(pos, miller, rot, shifts)


def backward_kernel(
    chunk, factor, nrefl, f_ref, obs_ref, wt_ref, pos_ref, mil_ref, rot_ref, shift_ref,
    amp_ref, grad_ref, w_ref,
):
    local = pos_ref.shape[1]
    nops = shift_ref.shape[0] // 3
    fa = jnp.sum(f_ref[:, 0, :], axis=0, keepdims=True)
    fb = jnp.sum(f_ref[:, 1, :], axis=0, keepdims=True)
    amp = jnp.sqrt(fa * fa + fb * fb + 1.0)
    amp_ref[...] = amp
    slope = 2.0 * wt_ref[...] * (amp - obs_ref[...]) / (amp * math.sqrt(nrefl))
    ga, gb = slope * fa, slope * fb
    total = jnp.zeros((KL, 4 * KP), jnp.float32)
    for s in range(nops):
        kl, h, flip, tc, ts = operator_terms(mil_ref, rot_ref, shift_ref, s)
        vre = tc * ga + ts * gb
        vim = flip * (ts * ga - tc * gb)
        pick = hot(h, KP)
        re_hi, re_lo = split2(jnp.where(pick, vre, 0.0))
        im_hi, im_lo = split2(jnp.where(pick, vim, 0.0))
        spread = jnp.concatenate([re_hi, im_hi, re_lo, im_lo], axis=0)
        total = total + lax.dot_general(as_bf16(hot(kl, KL)), spread, NT, preferred_element_type=jnp.float32)
    wre = total[:, 0:KP] + total[:, 2 * KP : 3 * KP]
    wim = total[:, KP : 2 * KP] + total[:, 3 * KP :]
    hval = (lax.broadcasted_iota(jnp.int32, (1, KP), 1) - MAXH).astype(jnp.float32)
    w_ref[0] = jnp.concatenate([wre, -wim], axis=1).astype(jnp.bfloat16)
    w_ref[1] = jnp.concatenate([wim, wre], axis=1).astype(jnp.bfloat16)
    w_ref[2] = jnp.concatenate([wre * hval, -wim * hval], axis=1).astype(jnp.bfloat16)
    w_ref[3] = jnp.concatenate([wim * hval, wre * hval], axis=1).astype(jnp.bfloat16)
    kval = (lax.broadcasted_iota(jnp.int32, (KP, chunk), 0) - MAXH).astype(jnp.float32)

    def evaluate(i, carry):
        cols = pl.ds(pl.multiple_of(i * chunk, chunk), chunk)
        xc, xs, yc, ys, zc, zs = tables(pos_ref, cols, chunk)
        xt = jnp.concatenate([xc, xs], axis=0).astype(jnp.bfloat16)
        acc = jnp.zeros((KP, chunk), jnp.float32)
        accx, accz = acc, acc
        for l in range(LP):
            rows = pl.ds(l * KP, KP)
            v = [jnp.dot(w_ref[j, rows, :], xt, preferred_element_type=jnp.float32) for j in range(4)]
            a, b = zc[l : l + 1], zs[l : l + 1]
            yzc = yc * a - ys * b
            yzs = yc * b + ys * a
            term = v[1] * yzc + v[0] * yzs
            acc = acc + term
            accx = accx + v[3] * yzc + v[2] * yzs
            accz = accz + float(l) * term
        scale = -factor * pos_ref[3:4, cols]
        grad_ref[0:1, cols] = scale * jnp.sum(accx, axis=0, keepdims=True)
        grad_ref[1:2, cols] = scale * jnp.sum(acc * kval, axis=0, keepdims=True)
        grad_ref[2:3, cols] = scale * jnp.sum(accz, axis=0, keepdims=True)
        return carry

    lax.fori_loop(0, local // chunk, evaluate, 0)


def backward(parts, observed, obs_weight, pos, miller, rot, shifts, factor, nrefl):
    local = pos.shape[1]
    group = miller.shape[1]
    return pl.pallas_call(
        functools.partial(backward_kernel, min(256, local), factor, nrefl),
        out_shape=(
            jax.ShapeDtypeStruct((1, group), jnp.float32),
            jax.ShapeDtypeStruct((3, local), jnp.float32),
        ),
        in_specs=[VMEM] * 5 + [SMEM, SMEM],
        out_specs=(VMEM, VMEM),
        scratch_shapes=[pltpu.VMEM((4, KL, 2 * KP), jnp.bfloat16)],
        compiler_params=pltpu.CompilerParams(vmem_limit_bytes=VLIM),
    )(parts, observed[None, :], obs_weight[None, :], pos, miller, rot, shifts)


def body(
    features,
    ln_gain,
    w_qkv,
    w_out,
    w_coord,
    noisy_coords,
    scatter_power,
    route,
    miller,
    rotations,
    shifts,
    observed,
    obs_weight,
):
    shards = lax.axis_size("atom")
    groups = lax.axis_size("refl")
    rank = lax.axis_index("atom")
    local, width = features.shape
    natom = local * shards
    group = miller.shape[1]
    nops = rotations.shape[0]
    nrefl = group * groups
    norm = 1.0 / math.sqrt(nops * natom)

    per_dev = w_qkv.shape[3] // HEAD_FEATURES
    wpack = w_qkv.reshape(LAYERS, 3, width, per_dev, HEAD_FEATURES).transpose(3, 0, 2, 1, 4)
    wpack = wpack.reshape(per_dev * LAYERS * width, 3 * HEAD_FEATURES)
    wpack = jnp.pad(wpack, ((0, 0), (0, 128 - 3 * HEAD_FEATURES)))
    wg, left, right = opening(wpack, features, 0)
    own_out, own_packed = attention(
        features, left, right, wg, ln_gain, w_out, w_coord, noisy_coords, scatter_power
    )
    atom_out = lax.all_gather(own_out, "refl", axis=0, tiled=True)
    packed = exchange(own_packed, "refl", 1, True).transpose(1, 0, 2).reshape(8, local)

    rot = rotations.reshape(-1)
    sh = shifts.reshape(-1)
    own_f = forward(packed, miller, rot, sh, norm)

    blk = local // shards
    routed = packed[:4].reshape(4, shards, blk)[:, route[0], :].transpose(1, 0, 2)
    routed = routed.reshape(shards, 4 * blk // 128, 128)
    mine = jnp.broadcast_to(own_f.reshape(1, 2 * group // 128, 128), (shards, 2 * group // 128, 128))
    came = exchange(jnp.concatenate([mine, routed], axis=1), "atom", 2, False)
    f_parts = came[:, : 2 * group // 128].reshape(shards, 2, group)
    pos = came[:, 2 * group // 128 :].reshape(shards, 4, blk).transpose(1, 0, 2).reshape(4, local)

    amp, grad = backward(
        f_parts, observed, obs_weight, pos, miller, rot, sh, 2.0 * math.pi * norm, nrefl
    )
    share = group // shards
    amplitude = lax.dynamic_slice_in_dim(amp[0], rank * share, share, 0)
    grads = exchange(grad.reshape(3 * local // 128, 128), "refl", 3, True)
    coord_grad = jnp.sum(grads, axis=0).reshape(3, local)
    return (atom_out, amplitude, coord_grad)


def solution(mesh):
    placed = (
        P("atom", None),
        P(),
        P(None, None, None, "refl"),
        P(),
        P(),
        P(None, "atom"),
        P("atom"),
        P("atom", None),
        P(None, "refl"),
        P(),
        P(),
        P("refl"),
        P("refl"),
    )
    return jax.shard_map(
        body,
        mesh=mesh,
        in_specs=placed,
        out_specs=(P("atom", None), P(("refl", "atom")), P(None, "atom")),
        check_vma=False,
    )
```
